256 devices in a mesh: loop: 4 (over y_hi, core), inner: 64 (over z, x, y_lo).
Axes of the slice: x: 4, y: 4 (y_hi: 2, y_lo: 2; y = y_hi * 2 + y_lo), z: 8, core: 2. Of those that a mesh axis runs over, the one named last changes fastest.
Arguments:
- snapshots: bfloat16 [65536, 1024], P(('loop', 'inner')), may hold values from -6 to 6
- bins: int32 [65536], replicated, may hold values from 0 to 511, as said below
- pairs: int32 [2048, 2], replicated, may hold values from 0 to 511, as said below
- start_weights: bfloat16 [1024, 32], replicated, may hold values from -0.1875 to 0.1875
Outputs:
- basis: float32 [65536, 96], P(('loop', 'inner'))
- coefficients: float32 [4, 32, 32], replicated
The draws below stay inside these ranges and needn't reach their ends.
Inputs may be any that keep to these rules, and one draw needn't show every extreme that they name: `bins`: the snapshot in row n has a bin in [r * 8, (r + 1) * 8), where r = (n // 256) mod (64). `pairs`: every row (a, b) has a <= b <= a + 8; every bin is paired with itself.
All inputs are finite; a program needn't handle non-finite values.
Results may differ from the reference program's by a relative error of at most 0.0003.
Values may be sent and summed in bfloat16 or wider, within the bound.
A program may use at most 64 MiB of HBM per device.

```python
import jax
import jax.numpy as jnp
from jax import lax

FEATURES = 1024
BLOCK = 32
STEPS = 2
BINS_COL = 8
LINKS = 4
ROWS_DEV = 256
SNAPSHOTS = 65536
NBINS = 512
PAIRS = 2048
N_LOOP = 4
N_INNER = 64


def draw_bins(key, part):
    index = jnp.arange(SNAPSHOTS, dtype=jnp.int32)
    column = index // ROWS_DEV % (NBINS // BINS_COL)
    within = index % ROWS_DEV
    first_key = jax.random.fold_in(key, 11)
    second_key = jax.random.fold_in(key, 12)
    first_pick = jax.random.randint(first_key, (SNAPSHOTS,), 0, BINS_COL, dtype=jnp.int32)
    second_pick = jax.random.randint(second_key, (SNAPSHOTS,), 0, BINS_COL, dtype=jnp.int32)
    offset = jnp.minimum(first_pick, second_pick)
    offset = jnp.where(within == 0, 0, jnp.where(within == ROWS_DEV - 1, BINS_COL - 1, offset))
    return (column * BINS_COL + offset).astype(jnp.int32)


def draw_pairs(key, part):
    index = jnp.arange(PAIRS, dtype=jnp.int32)
    anchor = index // LINKS
    link_index = index % LINKS
    offset = jax.random.randint(jax.random.fold_in(key, 21), (PAIRS,), 1, BINS_COL + 1, dtype=jnp.int32)
    offset = jnp.where(link_index == 0, 0, offset)
    target = jnp.minimum(anchor + offset, NBINS - 1)
    return jnp.stack([anchor, target], axis=1).astype(jnp.int32)


def block_levels(stream_key, extent, pieces, low, top_value):
    def one(dim, parts):
        draws = jax.random.uniform(jax.random.fold_in(jax.random.fold_in(stream_key, 6), dim), (parts,), jnp.float32, low / len(pieces), top_value / len(pieces))
        return jnp.repeat(jnp.exp(draws), extent[dim] // parts).reshape((-1,) + (1,) * (len(extent) - dim - 1))

    gain = one(*pieces[0])
    for cut in pieces[1:]:
        gain = gain * one(*cut)
    return gain


def normal_values(stream_key, shape, deviation, bound, shards=(), kind=jnp.bfloat16):
    entries = jax.random.normal(stream_key, shape, jnp.float32) * deviation
    if len(shards) > 0:
        entries = block_levels(stream_key, shape, shards, -0.22, 0.18) * entries
    return jnp.clip(entries, min=-bound, max=bound).astype(kind)


def setup_inputs(seed: int = 0) -> dict:
    key_of = jax.random.split(jax.random.key(seed), 5)
    snapshots = normal_values(key_of[0], (SNAPSHOTS, FEATURES), 1.0, 6.0, ((0, 256),))
    bins = draw_bins(jax.random.fold_in(key_of[4], 71), 0)
    pairs = draw_pairs(jax.random.fold_in(key_of[4], 71), 0)
    start_weights = normal_values(key_of[3], (FEATURES, BLOCK), FEATURES ** -0.5, 0.1875)
    return {"snapshots": snapshots, "bins": bins, "pairs": pairs, "start_weights": start_weights}


def gram_matrix(left, right):
    return jnp.dot(left.T, right, precision=lax.Precision.HIGHEST)

def orthonormal(matrix):
    lower_factor = jnp.linalg.cholesky(gram_matrix(matrix, matrix))
    result = lax.linalg.triangular_solve(lower_factor, matrix, left_side=False, lower=True, transpose_a=True)
    return (result, lower_factor.T)

def reference(snapshots, bins, pairs, start_weights):
    adjacency = jnp.zeros((NBINS, NBINS), jnp.float32)
    adjacency = adjacency.at[pairs[:, 0], pairs[:, 1]].set(1.0).at[pairs[:, 1], pairs[:, 0]].set(1.0)
    grid = snapshots.reshape(N_LOOP, N_INNER, ROWS_DEV, FEATURES)
    padded = jnp.pad(grid, ((0, 0), (1, 1), (0, 0), (0, 0)))
    bin_grid = jnp.pad(bins.reshape(N_LOOP, N_INNER, ROWS_DEV), ((0, 0), (1, 1), (0, 0)), constant_values=-1)
    epsilon = FEATURES / 3.0
    columns = jnp.arange(N_INNER, dtype=jnp.int32)

    def column_kernel(column):
        mine = lax.dynamic_index_in_dim(padded, column + 1, 1, keepdims=False).reshape(N_LOOP * ROWS_DEV, FEATURES)
        partner = lax.dynamic_slice_in_dim(padded, column, 3, 1).reshape(N_LOOP * 3 * ROWS_DEV, FEATURES)
        my_bins = lax.dynamic_index_in_dim(bin_grid, column + 1, 1, keepdims=False).reshape(-1)
        part_bins = lax.dynamic_slice_in_dim(bin_grid, column, 3, 1).reshape(-1)
        valid = (part_bins >= 0).astype(jnp.float32)
        linked = adjacency[my_bins][:, jnp.maximum(part_bins, 0)] * valid[None, :]
        mine_wide = mine.astype(jnp.float32)
        part_wide = partner.astype(jnp.float32)
        mine_norms = lax.optimization_barrier(jnp.sum(mine_wide * mine_wide, axis=1))
        part_norms = lax.optimization_barrier(jnp.sum(part_wide * part_wide, axis=1))
        products = jnp.dot(mine_wide, part_wide.T, precision=lax.Precision.HIGHEST)
        distance = mine_norms[:, None] + part_norms[None, :] - 2.0 * products
        return linked * jnp.exp(-distance / epsilon)

    def regroup(stacked):
        width = stacked.shape[-1]
        return stacked.reshape(N_INNER, N_LOOP, ROWS_DEV, width).transpose(1, 0, 2, 3).reshape(-1, width)

    def degree_column(column):
        return lax.optimization_barrier(jnp.sum(column_kernel(column), axis=1))[:, None]
    degree = regroup(lax.map(degree_column, columns))[:, 0]
    inv_root = lax.rsqrt(degree)

    def apply_kernel(vectors):
        width = vectors.shape[1]
        vec_pad = jnp.pad(vectors.reshape(N_LOOP, N_INNER, ROWS_DEV, width), ((0, 0), (1, 1), (0, 0), (0, 0)))

        def one_column(column):
            partner = lax.dynamic_slice_in_dim(vec_pad, column, 3, 1).reshape(N_LOOP * 3 * ROWS_DEV, width)
            return jnp.dot(column_kernel(column), partner, precision=lax.Precision.HIGHEST)
        return regroup(lax.map(one_column, columns))
    start_block = jnp.dot(snapshots.astype(jnp.float32), start_weights.astype(jnp.float32), preferred_element_type=jnp.float32)
    current, unused = orthonormal(start_block)
    basis_blocks = [current]
    coefficients = []
    previous = current
    prev_b = jnp.zeros((BLOCK, BLOCK), jnp.float32)
    for lanczos_step in range(STEPS):
        image = inv_root[:, None] * apply_kernel(inv_root[:, None] * current)
        projected = gram_matrix(current, image)
        image = image - jnp.dot(current, projected, precision=lax.Precision.HIGHEST)
        if lanczos_step > 0:
            image = image - jnp.dot(previous, prev_b.T, precision=lax.Precision.HIGHEST)
        following, factor = orthonormal(image)
        coefficients.append(projected)
        coefficients.append(factor)
        previous = current
        prev_b = factor
        current = following
        basis_blocks.append(current)
    return (jnp.concatenate(basis_blocks, axis=1), jnp.stack(coefficients))
```

```python
import functools

import jax
import jax.numpy as jnp
from jax import lax
from jax.experimental import pallas as pl
from jax.experimental.pallas import tpu as pltpu
from jax.sharding import PartitionSpec as P

MESH = pl.DeviceIdType.MESH
HIGHEST = lax.Precision.HIGHEST
F32 = jnp.float32
BF16 = jnp.bfloat16

NX, NY, NZ = 4, 4, 8
BINS_COL = 8
WINDOW = 32
ROWS = 256
BLOCK = 32
PARTNERS = 12
CHUNKS = 4
CHUNK = ROWS // CHUNKS
DIRECT = 1
HALF = ROWS // 2


def mm(a, b):
    return lax.dot_general(a, b, (((1,), (0,)), ((), ())), precision=HIGHEST, preferred_element_type=F32)


def mm_t(a, b):
    return lax.dot_general(a, b, (((1,), (1,)), ((), ())), precision=HIGHEST, preferred_element_type=F32)


def t_mm(a, b):
    return mm(a.T, b)


def split(v):
    high = v.astype(BF16)
    return high, (v - high.astype(F32)).astype(BF16)


def pack(m):
    return jnp.concatenate([m[8 * g : 8 * g + 8, :] for g in range(4)], axis=1)


def unpack(p):
    return jnp.concatenate([p[:, 32 * g : 32 * g + 32] for g in range(4)], axis=0)


def factorise(gram):
    sub = lax.broadcasted_iota(jnp.int32, (BLOCK, BLOCK), 0)
    lane = lax.broadcasted_iota(jnp.int32, (BLOCK, BLOCK), 1)
    eye = (sub == lane).astype(F32)
    work = jnp.concatenate([gram, eye], axis=1)
    below = lax.broadcasted_iota(jnp.int32, (BLOCK, 2 * BLOCK), 0)
    scale = jnp.zeros((BLOCK, 2 * BLOCK), F32)
    for k in range(BLOCK):
        row = jnp.broadcast_to(work[k : k + 1, :], (BLOCK, 2 * BLOCK))
        column = jnp.broadcast_to(work[:, k : k + 1], (BLOCK, 2 * BLOCK))
        pivot = jnp.broadcast_to(column[k : k + 1, :], (BLOCK, 2 * BLOCK))
        scale = jnp.where(below == k, pivot, scale)
        work = work - jnp.where(below > k, column / pivot, 0.0) * row
    work = work * lax.rsqrt(scale)
    upper = jnp.where(lane >= sub, work[:, :BLOCK], 0.0)
    return upper, work[:, BLOCK:]


def kernel(
    x_ref, bins_ref, pairs_ref, wt_ref, out_ref, coef_ref,
    xb, kh, kl, hot, links, st, sq_row, deg, irb, zb, vb, core_buf, plane_buf, line_buf,
    x_send, x_first, x_fwd, x_core, ir_sem, v_sem, ar_sem,
):
    features = x_ref.shape[1]
    group = lax.axis_index("loop")
    inner = lax.axis_index("inner")
    core = group % 2
    odd = inner % 2
    y = (group // 2) * 2 + odd
    x = (inner // 2) % NX
    z = inner // (2 * NX)

    def device(c, xx, yy, zz):
        yy = yy % NY
        return ((yy // 2) * 2 + c, (zz % NZ) * (2 * NX) + (xx % NX) * 2 + yy % 2)

    def near(dc, dy, di):
        yy = (y + dy) % NY
        return ((yy // 2) * 2 + (core + dc) % 2, ((inner // 2 + di) % (NX * NZ)) * 2 + yy % 2)

    step = 1 - 2 * odd
    other = near(1, 0, 0)

    barrier = pltpu.get_barrier_semaphore()
    greeted = [other]
    greeted += [device(core, x + a, y + b, z) for a in range(NX) for b in range(NY) if a or b]
    greeted += [device(core, x, y, z + a) for a in range(1, NZ)]
    greeted += [near(1, dy, 0) for dy in (1, 2, 3)]
    greeted += [near(dc, dy, -step) for dc in (0, 1) for dy in (1, 3)]
    greeted += [near(0, 0, 1), near(0, 0, -1)]
    for d in greeted:
        pl.semaphore_signal(barrier, inc=1, device_id=d, device_id_type=MESH)
    pl.semaphore_wait(barrier, len(greeted))

    def remote(src, dst, send, recv, target):
        return pltpu.make_async_remote_copy(
            src_ref=src, dst_ref=dst, send_sem=send, recv_sem=recv, device_id=target, device_id_type=MESH
        )

    def rows_of(chunk):
        return pl.ds(chunk * CHUNK, CHUNK)

    def push(src, slot, chunk, recv, target):
        source = x_ref.at[rows_of(chunk)] if src is None else xb.at[src, rows_of(chunk)]
        remote(source, xb.at[slot, rows_of(chunk)], x_send, recv, target).start()

    def arrived(ref, sem):
        pltpu.make_async_copy(ref, ref, sem).wait()

    up = list(range(CHUNKS))
    down = up[CHUNKS // 2 :] + up[: CHUNKS // 2]
    far_up, far_down = up[CHUNKS - DIRECT :], down[CHUNKS - DIRECT :]
    for k in range(CHUNKS):
        push(None, 3, up[k], x_first.at[1, up[k]], near(0, 1, 0))
        push(None, 2, down[k], x_first.at[0, down[k]], near(0, -1, 0))
        if k < DIRECT:
            push(None, 6, far_up[k], x_first.at[4, far_up[k]], near(0, 1, -step))
            push(None, 5, far_down[k], x_first.at[3, far_down[k]], near(0, -1, -step))
    remote(x_ref, xb.at[1], x_send, x_core.at[0, 0], other).start()

    def sum_start(n, packed):
        rows = packed.shape[0]
        core_buf[n, 0, pl.ds(0, rows)] = packed
        remote(
            core_buf.at[n, 0, pl.ds(0, rows)], core_buf.at[n, 1, pl.ds(0, rows)],
            ar_sem.at[n, 0], ar_sem.at[n, 1], other,
        ).start()

    def sum_plane(n, rows):
        arrived(core_buf.at[n, 1, pl.ds(0, rows)], ar_sem.at[n, 1])
        both = core_buf[n, 0, pl.ds(0, rows)] + core_buf[n, 1, pl.ds(0, rows)]
        mine = x * NY + y
        plane_buf[n, mine, pl.ds(0, rows)] = both
        place = plane_buf.at[n, mine, pl.ds(0, rows)]

        def send(k, carry):
            remote(
                place, place, ar_sem.at[n, 2], ar_sem.at[n, 3], device(core, x + k // NY, y + k % NY, z)
            ).start()
            return carry

        lax.fori_loop(1, NX * NY, send, 0)

    def sum_line(n, rows):
        span = plane_buf.at[n, pl.ds(0, NX * NY - 1), pl.ds(0, rows)]
        arrived(span, ar_sem.at[n, 3])
        total = jnp.sum(plane_buf[n, :, pl.ds(0, rows)], axis=0)
        line_buf[n, z, pl.ds(0, rows)] = total
        place = line_buf.at[n, z, pl.ds(0, rows)]

        def send(k, carry):
            remote(place, place, ar_sem.at[n, 4], ar_sem.at[n, 5], device(core, x, y, z + k)).start()
            return carry

        lax.fori_loop(1, NZ, send, 0)

    def sum_end(n, rows):
        arrived(line_buf.at[n, pl.ds(0, NZ - 1), pl.ds(0, rows)], ar_sem.at[n, 5])
        return jnp.sum(line_buf[n, :, pl.ds(0, rows)], axis=0)

    def sum_drain(n, rows):
        arrived(core_buf.at[n, 0, pl.ds(0, rows)], ar_sem.at[n, 0])
        arrived(plane_buf.at[n, pl.ds(0, NX * NY - 1), pl.ds(0, rows)], ar_sem.at[n, 2])
        arrived(line_buf.at[n, pl.ds(0, NZ - 1), pl.ds(0, rows)], ar_sem.at[n, 4])

    own = x_ref[...]
    wt = wt_ref[...]
    start = lax.dot_general(wt, own, (((1,), (1,)), ((), ())), preferred_element_type=F32)
    st[:, pl.ds(0, ROWS)] = start
    sum_start(0, pack(mm_t(start, start)))

    pairs = pairs_ref[...]
    left, right = pairs[0:1, :], pairs[1:2, :]
    count = pairs.shape[1]
    my_base = inner * BINS_COL
    window_base = my_base - BINS_COL

    def one_hot(values, base, width):
        ids = lax.broadcasted_iota(jnp.int32, (width, values.shape[1]), 0)
        return jnp.where(values - base == ids, 1.0, 0.0).astype(F32)

    def count_pairs(mine, theirs):
        return lax.dot_general(
            one_hot(mine, my_base, BINS_COL).astype(BF16), one_hot(theirs, window_base, WINDOW).astype(BF16),
            (((1,), (1,)), ((), ())), preferred_element_type=F32,
        )

    linked = jnp.where(count_pairs(left, right) + count_pairs(right, left) > 0.5, 1.0, 0.0)

    def bins_of(block):
        eight = bins_ref[pl.ds(pl.multiple_of((block // 4) * 8, 8), 8), :]
        which = lax.broadcasted_iota(jnp.int32, eight.shape, 0) - 2 * (block % 4)
        first = jnp.sum(jnp.where(which == 0, eight, 0), axis=0, keepdims=True)
        second = jnp.sum(jnp.where(which == 1, eight, 0), axis=0, keepdims=True)
        return jnp.concatenate([first, second], axis=1)

    n_inner = NX * NZ * 2
    my_bins = bins_of(group * n_inner + inner)
    links[...] = mm(linked.T, one_hot(my_bins, my_base, BINS_COL)).astype(BF16)

    def set_hot(slot, where, valid):
        hits = one_hot(bins_of(where[0] * n_inner + where[1]), window_base, WINDOW)
        if valid is not None:
            hits = hits * valid
        hot[slot] = hits.T.astype(BF16)

    across = jnp.where((inner == 0) | (inner == n_inner - 1), 0.0, 1.0).astype(F32)
    set_hot(0, (group, inner), None)
    set_hot(1, other, None)
    for dc in (0, 1):
        for slot, dy in ((2, 1), (3, -1), (4, 2)):
            set_hot(slot + 5 * dc, near(dc, dy, 0), None)
        for slot, dy in ((5, 1), (6, -1)):
            set_hot(slot + 5 * dc, near(dc, dy, -step), across)

    wide = own.astype(F32)
    sq_high, sq_low = split(wide * wide)
    ones = jnp.ones((16, features), BF16)
    norms = lax.dot_general(ones, sq_high, (((1,), (1,)), ((), ())), preferred_element_type=F32)
    norms = norms + lax.dot_general(ones, sq_low, (((1,), (1,)), ((), ())), preferred_element_type=F32)
    sq_row[...] = norms[0:8, :]
    xb[0] = own
    deg[...] = jnp.zeros_like(deg)

    def tile(slot, half):
        span = pl.ds(pl.multiple_of(half * HALF, HALF), HALF)
        theirs = xb[slot, span, :]
        theirs_wide = theirs.astype(F32)
        their_norm = jnp.sum(theirs_wide * theirs_wide, axis=1, keepdims=True)
        products = lax.dot_general(theirs, x_ref[...], (((1,), (1,)), ((), ())), preferred_element_type=F32)
        distance = their_norm + sq_row[0:1, :] - 2.0 * products
        mask = jnp.dot(hot[slot, span, :], links[...], preferred_element_type=F32)
        value = mask * jnp.exp(distance * (-3.0 / features))
        deg[...] += jnp.sum(value.reshape(HALF // 8, 8, ROWS), axis=0)
        high, low = split(value)
        kh[slot, span, :] = high
        kl[slot, span, :] = low

    def whole(slot):
        tile(slot, 0)
        tile(slot, 1)

    def image(slot):
        return lax.dot_general(wt_ref[...], xb[slot], (((1,), (1,)), ((), ())), preferred_element_type=F32)

    def forward(slot, chunk, target_slot, recv, target):
        push(slot, target_slot, chunk, recv, target)

    def got(slot, chunk):
        arrived(xb.at[slot, rows_of(chunk)], x_first.at[slot - 2, chunk])

    def to_core(slot, half):
        span = pl.ds(half * HALF, HALF)
        remote(xb.at[slot, span], xb.at[slot + 5, span], x_send, x_fwd.at[slot - 2, half], other).start()

    def got_core(slot, half):
        arrived(xb.at[slot, pl.ds(half * HALF, HALF)], x_fwd.at[slot - 7, half])

    sum_plane(0, 8)
    whole(0)
    arrived(xb.at[1], x_core.at[0, 0])
    whole(1)

    per = CHUNKS // 2
    for k in range(CHUNKS):
        a, b = down[k], up[k]
        got(2, a)
        if k < CHUNKS - DIRECT:
            push(2, 5, a, x_first.at[3, a], near(0, 0, step))
        if k < per:
            push(2, 4, a, x_first.at[2, a], near(0, -1, 0))
        got(3, b)
        if k < CHUNKS - DIRECT:
            push(3, 6, b, x_first.at[4, b], near(0, 0, step))
        if k < per:
            push(3, 4, b, x_first.at[2, b], near(0, 1, 0))
        if k % per == per - 1:
            to_core(2, a // per)
            to_core(3, b // per)
            tile(2, a // per)
            tile(3, b // per)
    sum_line(0, 8)
    for h in (0, 1):
        for s, halves in ((7, (1, 0)), (8, (0, 1))):
            got_core(s, halves[h])
            tile(s, halves[h])
    for h in (0, 1):
        for chunk in range(per * h, per * h + per):
            got(4, chunk)
        to_core(4, h)
        tile(4, h)
    for h in (0, 1):
        for s, halves in ((5, (1, 0)), (6, (0, 1))):
            for chunk in range(per * halves[h], per * halves[h] + per):
                got(s, chunk)
            to_core(s, halves[h])
            tile(s, halves[h])
        got_core(9, h)
        tile(9, h)
    for h in (0, 1):
        for s, halves in ((10, (1, 0)), (11, (0, 1))):
            got_core(s, halves[h])
            tile(s, halves[h])

    degree = jnp.sum(deg[...], axis=0, keepdims=True)
    root = lax.rsqrt(degree)
    irb[0] = root

    def to_partners(buf, send, recv):
        place = buf.at[0]
        remote(place, buf.at[1], send, recv, other).start()
        for dc in (0, 1):
            for slot, dy in ((3, 1), (2, -1), (4, 2)):
                remote(place, buf.at[slot + 5 * dc], send, recv, near(dc, dy, 0)).start()
            for slot, dy in ((6, 1), (5, -1)):
                remote(place, buf.at[slot + 5 * dc], send, recv, near(dc, dy, -step)).start()

    others = pl.ds(1, PARTNERS - 1)
    to_partners(irb, ir_sem.at[0], ir_sem.at[1])

    for slot in range(1, PARTNERS):
        st[:, pl.ds(slot * ROWS, ROWS)] = image(slot)
    unused, inverse = factorise(unpack(sum_end(0, 8)))
    st[...] = mm(inverse, st[...])
    q0 = st[:, pl.ds(0, ROWS)]
    out_ref[pl.ds(0, BLOCK), :] = q0

    arrived(irb.at[others], ir_sem.at[1])
    for slot in range(PARTNERS):
        high, low = split(st[:, pl.ds(slot * ROWS, ROWS)] * irb[slot])
        zb[slot, pl.ds(0, BLOCK), :] = high
        zb[slot, pl.ds(BLOCK, BLOCK), :] = low

    def apply(buf):
        total = jnp.zeros((2 * BLOCK, ROWS), F32)
        rest = jnp.zeros((BLOCK, ROWS), F32)
        for slot in range(PARTNERS):
            vectors = buf[slot]
            total = total + jnp.dot(vectors, kh[slot], preferred_element_type=F32)
            rest = rest + jnp.dot(vectors[:BLOCK, :], kl[slot], preferred_element_type=F32)
        return (total[:BLOCK, :] + (total[BLOCK:, :] + rest)) * irb[0]

    w0 = apply(zb)
    u0 = w0 - q0
    high, low = split(u0 * irb[0])
    vb[0, pl.ds(0, BLOCK), :] = high
    vb[0, pl.ds(BLOCK, BLOCK), :] = low
    moments = mm_t(jnp.concatenate([q0, u0], axis=0), u0)
    sum_start(1, jnp.concatenate([pack(moments[:BLOCK, :]), pack(moments[BLOCK:, :])], axis=0))
    to_partners(vb, v_sem.at[0], v_sem.at[1])
    sum_plane(1, 16)
    sum_line(1, 16)
    arrived(vb.at[others], v_sem.at[1])
    v2 = apply(vb)

    def eye():
        shape = (BLOCK, BLOCK)
        same = lax.broadcasted_iota(jnp.int32, shape, 0) == lax.broadcasted_iota(jnp.int32, shape, 1)
        return jnp.where(same, 1.0, 0.0).astype(F32)

    summed = sum_end(1, 16)
    e0 = unpack(summed[:8, :])
    e0_t = e0.T
    coef_ref[0] = e0 + eye()
    b0, inverse = factorise(unpack(summed[8:, :]) - mm(e0_t, e0))
    coef_ref[1] = b0
    pair = jnp.concatenate([u0, v2], axis=1) - mm(e0_t, jnp.concatenate([q0, w0], axis=1))
    pair = mm(inverse, pair)
    q1 = pair[:, :ROWS]
    out_ref[pl.ds(BLOCK, BLOCK), :] = q1
    u1 = pair[:, ROWS:] - mm(b0, q0) - q1
    moments = mm_t(jnp.concatenate([q1, u1], axis=0), u1)
    sum_start(2, jnp.concatenate([pack(moments[:BLOCK, :]), pack(moments[BLOCK:, :])], axis=0))
    sum_plane(2, 16)
    sum_line(2, 16)

    arrived(xb.at[pl.ds(0, PARTNERS - 1)], x_send)
    arrived(irb.at[others], ir_sem.at[0])
    arrived(vb.at[others], v_sem.at[0])
    sum_drain(0, 8)
    sum_drain(1, 16)

    summed = sum_end(2, 16)
    e1 = unpack(summed[:8, :])
    e1_t = e1.T
    coef_ref[2] = e1 + eye()
    b1, inverse = factorise(unpack(summed[8:, :]) - mm(e1_t, e1))
    coef_ref[3] = b1
    out_ref[pl.ds(2 * BLOCK, BLOCK), :] = mm(inverse, u1 - mm(e1_t, q1))
    sum_drain(2, 16)


def local(snapshots, bins, pairs, start_weights):
    rows, features = snapshots.shape
    vmem = pl.BlockSpec(memory_space=pltpu.VMEM)
    basis, coefficients = pl.pallas_call(
        kernel,
        out_shape=(
            jax.ShapeDtypeStruct((3 * BLOCK, rows), F32),
            jax.ShapeDtypeStruct((4, BLOCK, BLOCK), F32),
        ),
        in_specs=[vmem] * 4,
        out_specs=(vmem, vmem),
        scratch_shapes=[
            pltpu.VMEM((PARTNERS, rows, features), BF16),
            pltpu.VMEM((PARTNERS, rows, rows), BF16),
            pltpu.VMEM((PARTNERS, rows, rows), BF16),
            pltpu.VMEM((PARTNERS, rows, WINDOW), BF16),
            pltpu.VMEM((WINDOW, rows), BF16),
            pltpu.VMEM((BLOCK, PARTNERS * rows), F32),
            pltpu.VMEM((8, rows), F32),
            pltpu.VMEM((8, rows), F32),
            pltpu.VMEM((PARTNERS, 1, rows), F32),
            pltpu.VMEM((PARTNERS, 2 * BLOCK, rows), BF16),
            pltpu.VMEM((PARTNERS, 2 * BLOCK, rows), BF16),
            pltpu.VMEM((3, 2, 16, 128), F32),
            pltpu.VMEM((3, NX * NY, 16, 128), F32),
            pltpu.VMEM((3, NZ, 16, 128), F32),
            pltpu.SemaphoreType.DMA,
            pltpu.SemaphoreType.DMA((5, CHUNKS)),
            pltpu.SemaphoreType.DMA((5, 2)),
            pltpu.SemaphoreType.DMA((1, 1)),
            pltpu.SemaphoreType.DMA((2,)),
            pltpu.SemaphoreType.DMA((2,)),
            pltpu.SemaphoreType.DMA((3, 6)),
        ],
        compiler_params=pltpu.CompilerParams(
            collective_id=0, has_side_effects=True, vmem_limit_bytes=48 << 20
        ),
    )(snapshots, bins.reshape(-1, 128), pairs.T, start_weights.T)
    return basis.T, coefficients


def solution(mesh):
    in_specs = (P(("loop", "inner"), None), P(), P(), P())
    out_specs = (P(("loop", "inner"), None), P())
    return jax.shard_map(local, mesh=mesh, in_specs=in_specs, out_specs=out_specs, check_vma=False)
```

```python
import functools

import jax
import jax.numpy as jnp
from jax import lax
from jax.experimental import pallas as pl
from jax.experimental.pallas import tpu as pltpu
from jax.sharding import PartitionSpec as P

MESH = pl.DeviceIdType.MESH
HIGHEST = lax.Precision.HIGHEST
F32 = jnp.float32
BF16 = jnp.bfloat16

NX, NY, NZ = 4, 4, 8
BINS_COL = 8
WINDOW = 32
ROWS = 256
BLOCK = 32
PARTNERS = 12
CHUNKS = 8
CHUNK = ROWS // CHUNKS
DIRECT = 3
HALF = ROWS // 2


def mm(a, b):
    return lax.dot_general(a, b, (((1,), (0,)), ((), ())), precision=HIGHEST, preferred_element_type=F32)


def mm_t(a, b):
    return lax.dot_general(a, b, (((1,), (1,)), ((), ())), precision=HIGHEST, preferred_element_type=F32)


def t_mm(a, b):
    return mm(a.T, b)


def split(v):
    high = v.astype(BF16)
    return high, (v - high.astype(F32)).astype(BF16)


def pack(m):
    return jnp.concatenate([m[8 * g : 8 * g + 8, :] for g in range(4)], axis=1)


def unpack(p):
    return jnp.concatenate([p[:, 32 * g : 32 * g + 32] for g in range(4)], axis=0)


def factorise(gram):
    sub = lax.broadcasted_iota(jnp.int32, (BLOCK, BLOCK), 0)
    lane = lax.broadcasted_iota(jnp.int32, (BLOCK, BLOCK), 1)
    eye = (sub == lane).astype(F32)
    work = jnp.concatenate([gram, eye], axis=1)
    below = lax.broadcasted_iota(jnp.int32, (BLOCK, 2 * BLOCK), 0)
    scale = jnp.zeros((BLOCK, 2 * BLOCK), F32)
    for k in range(0, BLOCK, 2):
        first = jnp.broadcast_to(work[:, k : k + 1], (BLOCK, 2 * BLOCK))
        second = jnp.broadcast_to(work[:, k + 1 : k + 2], (BLOCK, 2 * BLOCK))
        row, next_row = work[k : k + 1, :], work[k + 1 : k + 2, :]
        pivot, cross = first[k : k + 1, :], second[k : k + 1, :]
        inverse = 1.0 / pivot
        ratio = first[k + 1 : k + 2, :] * inverse
        next_row = next_row - ratio * row
        next_pivot = second[k + 1 : k + 2, :] - ratio * cross
        second = second - first * (cross * inverse)
        change = first * (row * inverse) + second * (next_row * (1.0 / next_pivot))
        scale = jnp.where(below == k, pivot, jnp.where(below == k + 1, next_pivot, scale))
        work = jnp.where(below == k + 1, next_row, work) - jnp.where(below > k + 1, change, 0.0)
    work = work * lax.rsqrt(scale)
    upper = jnp.where(lane >= sub, work[:, :BLOCK], 0.0)
    return upper, work[:, BLOCK:]


def kernel(
    x_hbm, bins_hbm, pairs_hbm, wt_hbm, out_ref, coef_ref,
    bins_ref, pairs_ref, wt_ref, xb, kh, kl, hot, links, st, sq_row, deg, irb, zb, vb, core_buf, plane_buf, line_buf,
    x_send, x_first, x_fwd, x_core, ir_sem, v_sem, ar_sem, in_sem,
):
    x_ref = xb.at[0]
    arrivals = [
        pltpu.make_async_copy(src, dst, in_sem.at[n])
        for n, (src, dst) in enumerate(
            ((x_hbm, x_ref), (wt_hbm, wt_ref), (pairs_hbm, pairs_ref), (bins_hbm, bins_ref))
        )
    ]
    for copy in arrivals:
        copy.start()
    features = xb.shape[2]
    group = lax.axis_index("loop")
    inner = lax.axis_index("inner")
    core = group % 2
    odd = inner % 2
    y = (group // 2) * 2 + odd
    x = (inner // 2) % NX
    z = inner // (2 * NX)

    def device(c, xx, yy, zz):
        yy = yy % NY
        return ((yy // 2) * 2 + c, (zz % NZ) * (2 * NX) + (xx % NX) * 2 + yy % 2)

    def near(dc, dy, di):
        yy = (y + dy) % NY
        return ((yy // 2) * 2 + (core + dc) % 2, ((inner // 2 + di) % (NX * NZ)) * 2 + yy % 2)

    step = 1 - 2 * odd
    other = near(1, 0, 0)

    barrier = pltpu.get_barrier_semaphore()
    greeted = [other]
    greeted += [device(core, x + a, y + b, z) for a in range(NX) for b in range(NY) if a or b]
    greeted += [device(core, x, y, z + a) for a in range(1, NZ)]
    greeted += [near(1, dy, 0) for dy in (1, 2, 3)]
    greeted += [near(dc, dy, -step) for dc in (0, 1) for dy in (1, 3)]
    greeted += [near(0, 0, 1), near(0, 0, -1)]
    for d in greeted:
        pl.semaphore_signal(barrier, inc=1, device_id=d, device_id_type=MESH)
    pl.semaphore_wait(barrier, len(greeted))
    arrivals[0].wait()

    def remote(src, dst, send, recv, target):
        return pltpu.make_async_remote_copy(
            src_ref=src, dst_ref=dst, send_sem=send, recv_sem=recv, device_id=target, device_id_type=MESH
        )

    def rows_of(chunk):
        return pl.ds(chunk * CHUNK, CHUNK)

    def push(src, slot, chunk, recv, target):
        source = x_ref.at[rows_of(chunk)] if src is None else xb.at[src, rows_of(chunk)]
        remote(source, xb.at[slot, rows_of(chunk)], x_send, recv, target).start()

    def arrived(ref, sem):
        pltpu.make_async_copy(ref, ref, sem).wait()

    up = list(range(CHUNKS))
    down = up[CHUNKS // 2 :] + up[: CHUNKS // 2]
    far_up, far_down = up[CHUNKS - DIRECT :], down[CHUNKS - DIRECT :]
    for k in range(CHUNKS):
        push(None, 3, up[k], x_first.at[1, up[k]], near(0, 1, 0))
        push(None, 2, down[k], x_first.at[0, down[k]], near(0, -1, 0))
        if k < DIRECT:
            push(None, 6, far_up[k], x_first.at[4, far_up[k]], near(0, 1, -step))
            push(None, 5, far_down[k], x_first.at[3, far_down[k]], near(0, -1, -step))
    remote(x_ref, xb.at[1], x_send, x_core.at[0, 0], other).start()

    def sum_start(n, packed):
        rows = packed.shape[0]
        core_buf[n, 0, pl.ds(0, rows)] = packed
        remote(
            core_buf.at[n, 0, pl.ds(0, rows)], core_buf.at[n, 1, pl.ds(0, rows)],
            ar_sem.at[n, 0], ar_sem.at[n, 1], other,
        ).start()

    def sum_plane(n, rows):
        arrived(core_buf.at[n, 1, pl.ds(0, rows)], ar_sem.at[n, 1])
        both = core_buf[n, 0, pl.ds(0, rows)] + core_buf[n, 1, pl.ds(0, rows)]
        mine = x * NY + y
        plane_buf[n, mine, pl.ds(0, rows)] = both
        place = plane_buf.at[n, mine, pl.ds(0, rows)]

        def send(k, carry):
            remote(
                place, place, ar_sem.at[n, 2], ar_sem.at[n, 3], device(core, x + k // NY, y + k % NY, z)
            ).start()
            return carry

        lax.fori_loop(1, NX * NY, send, 0)

    def sum_line(n, rows):
        span = plane_buf.at[n, pl.ds(0, NX * NY - 1), pl.ds(0, rows)]
        arrived(span, ar_sem.at[n, 3])
        total = jnp.sum(plane_buf[n, :, pl.ds(0, rows)], axis=0)
        line_buf[n, z, pl.ds(0, rows)] = total
        place = line_buf.at[n, z, pl.ds(0, rows)]

        def send(k, carry):
            remote(place, place, ar_sem.at[n, 4], ar_sem.at[n, 5], device(core, x, y, z + k)).start()
            return carry

        lax.fori_loop(1, NZ, send, 0)

    def sum_end(n, rows):
        arrived(line_buf.at[n, pl.ds(0, NZ - 1), pl.ds(0, rows)], ar_sem.at[n, 5])
        return jnp.sum(line_buf[n, :, pl.ds(0, rows)], axis=0)

    def sum_drain(n, rows):
        arrived(core_buf.at[n, 0, pl.ds(0, rows)], ar_sem.at[n, 0])
        arrived(plane_buf.at[n, pl.ds(0, NX * NY - 1), pl.ds(0, rows)], ar_sem.at[n, 2])
        arrived(line_buf.at[n, pl.ds(0, NZ - 1), pl.ds(0, rows)], ar_sem.at[n, 4])

    for copy in arrivals[1:]:
        copy.wait()

    own = x_ref[...]
    wt = wt_ref[...]
    start = lax.dot_general(wt, own, (((1,), (1,)), ((), ())), preferred_element_type=F32)
    sum_start(0, pack(mm_t(start, start)))

    pairs = pairs_ref[...]
    left, right = pairs[0:1, :], pairs[1:2, :]
    count = pairs.shape[1]
    my_base = inner * BINS_COL
    window_base = my_base - BINS_COL

    def one_hot(values, base, width):
        ids = lax.broadcasted_iota(jnp.int32, (width, values.shape[1]), 0)
        return jnp.where(values - base == ids, 1.0, 0.0).astype(F32)

    def count_pairs(mine, theirs):
        return lax.dot_general(
            one_hot(mine, my_base, BINS_COL).astype(BF16), one_hot(theirs, window_base, WINDOW).astype(BF16),
            (((1,), (1,)), ((), ())), preferred_element_type=F32,
        )

    linked = jnp.where(count_pairs(left, right) + count_pairs(right, left) > 0.5, 1.0, 0.0)

    def bins_of(block):
        eight = bins_ref[pl.ds(pl.multiple_of((block // 4) * 8, 8), 8), :]
        which = lax.broadcasted_iota(jnp.int32, eight.shape, 0) - 2 * (block % 4)
        first = jnp.sum(jnp.where(which == 0, eight, 0), axis=0, keepdims=True)
        second = jnp.sum(jnp.where(which == 1, eight, 0), axis=0, keepdims=True)
        return jnp.concatenate([first, second], axis=1)

    n_inner = NX * NZ * 2
    my_bins = bins_of(group * n_inner + inner)
    links[...] = mm(linked.T, one_hot(my_bins, my_base, BINS_COL)).astype(BF16)

    def set_hot(slot, where, valid):
        hits = one_hot(bins_of(where[0] * n_inner + where[1]), window_base, WINDOW)
        if valid is not None:
            hits = hits * valid
        hot[slot] = hits.T.astype(BF16)

    across = jnp.where((inner == 0) | (inner == n_inner - 1), 0.0, 1.0).astype(F32)
    set_hot(0, (group, inner), None)
    set_hot(1, other, None)
    for dc in (0, 1):
        for slot, dy in ((2, 1), (3, -1), (4, 2)):
            set_hot(slot + 5 * dc, near(dc, dy, 0), None)
        for slot, dy in ((5, 1), (6, -1)):
            set_hot(slot + 5 * dc, near(dc, dy, -step), across)

    wide = own.astype(F32)
    sq_high, sq_low = split(wide * wide)
    ones = jnp.ones((16, features), BF16)
    norms = lax.dot_general(ones, sq_high, (((1,), (1,)), ((), ())), preferred_element_type=F32)
    norms = norms + lax.dot_general(ones, sq_low, (((1,), (1,)), ((), ())), preferred_element_type=F32)
    sq_row[...] = norms[0:8, :]
    deg[...] = jnp.zeros_like(deg)

    def tile(slot, half):
        span = pl.ds(pl.multiple_of(half * HALF, HALF), HALF)
        theirs = xb[slot, span, :]
        theirs_wide = theirs.astype(F32)
        their_norm = jnp.sum(theirs_wide * theirs_wide, axis=1, keepdims=True)
        products = lax.dot_general(theirs, x_ref[...], (((1,), (1,)), ((), ())), preferred_element_type=F32)
        distance = their_norm + sq_row[0:1, :] - 2.0 * products
        mask = jnp.dot(hot[slot, span, :], links[...], preferred_element_type=F32)
        value = mask * jnp.exp(distance * (-3.0 / features))
        deg[...] += jnp.sum(value.reshape(HALF // 8, 8, ROWS), axis=0)
        high, low = split(value)
        kh[slot, span, :] = high
        kl[slot, span, :] = low
        st[:, pl.ds(slot * ROWS + half * HALF, HALF)] = lax.dot_general(
            wt_ref[...], theirs, (((1,), (1,)), ((), ())), preferred_element_type=F32
        )

    def whole(slot):
        tile(slot, 0)
        tile(slot, 1)

    def forward(slot, chunk, target_slot, recv, target):
        push(slot, target_slot, chunk, recv, target)

    def got(slot, chunk):
        arrived(xb.at[slot, rows_of(chunk)], x_first.at[slot - 2, chunk])

    def to_core(slot, half):
        span = pl.ds(half * HALF, HALF)
        remote(xb.at[slot, span], xb.at[slot + 5, span], x_send, x_fwd.at[slot - 2, half], other).start()

    def got_core(slot, half):
        arrived(xb.at[slot, pl.ds(half * HALF, HALF)], x_fwd.at[slot - 7, half])

    sum_plane(0, 8)
    whole(0)
    arrived(xb.at[1], x_core.at[0, 0])
    whole(1)

    per = CHUNKS // 2
    for k in range(CHUNKS):
        a, b = down[k], up[k]
        got(2, a)
        if k < CHUNKS - DIRECT:
            push(2, 5, a, x_first.at[3, a], near(0, 0, step))
        if k < per:
            push(2, 4, a, x_first.at[2, a], near(0, -1, 0))
        got(3, b)
        if k < CHUNKS - DIRECT:
            push(3, 6, b, x_first.at[4, b], near(0, 0, step))
        if k < per:
            push(3, 4, b, x_first.at[2, b], near(0, 1, 0))
        if k % per == per - 1:
            to_core(2, a // per)
            to_core(3, b // per)
            tile(2, a // per)
            tile(3, b // per)
    sum_line(0, 8)
    for h in (0, 1):
        for s, halves in ((7, (1, 0)), (8, (0, 1))):
            got_core(s, halves[h])
            tile(s, halves[h])
    for h in (0, 1):
        for chunk in range(per * h, per * h + per):
            got(4, chunk)
        to_core(4, h)
        tile(4, h)
    for h in (0, 1):
        for s, halves in ((5, (1, 0)), (6, (0, 1))):
            for chunk in range(per * halves[h], per * halves[h] + per):
                got(s, chunk)
            to_core(s, halves[h])
            tile(s, halves[h])
        got_core(9, h)
        tile(9, h)
    for h in (0, 1):
        for s, halves in ((10, (1, 0)), (11, (0, 1))):
            got_core(s, halves[h])
            tile(s, halves[h])

    degree = jnp.sum(deg[...], axis=0, keepdims=True)
    root = lax.rsqrt(degree)
    irb[0] = root

    def to_partners(buf, send, recv):
        place = buf.at[0]
        remote(place, buf.at[1], send, recv, other).start()
        for dc in (0, 1):
            for slot, dy in ((3, 1), (2, -1), (4, 2)):
                remote(place, buf.at[slot + 5 * dc], send, recv, near(dc, dy, 0)).start()
            for slot, dy in ((6, 1), (5, -1)):
                remote(place, buf.at[slot + 5 * dc], send, recv, near(dc, dy, -step)).start()

    others = pl.ds(1, PARTNERS - 1)
    to_partners(irb, ir_sem.at[0], ir_sem.at[1])

    unused, inverse = factorise(unpack(sum_end(0, 8)))
    st[...] = mm(inverse, st[...])
    q0 = st[:, pl.ds(0, ROWS)]
    out_ref[pl.ds(0, BLOCK), :] = q0

    arrived(irb.at[others], ir_sem.at[1])
    for slot in range(PARTNERS):
        high, low = split(st[:, pl.ds(slot * ROWS, ROWS)] * irb[slot])
        zb[slot, pl.ds(0, BLOCK), :] = high
        zb[slot, pl.ds(BLOCK, BLOCK), :] = low

    def apply(buf):
        total = jnp.zeros((2 * BLOCK, ROWS), F32)
        rest = jnp.zeros((BLOCK, ROWS), F32)
        for slot in range(PARTNERS):
            vectors = buf[slot]
            total = total + jnp.dot(vectors, kh[slot], preferred_element_type=F32)
            rest = rest + jnp.dot(vectors[:BLOCK, :], kl[slot], preferred_element_type=F32)
        return (total[:BLOCK, :] + (total[BLOCK:, :] + rest)) * irb[0]

    w0 = apply(zb)
    u0 = w0 - q0
    high, low = split(u0 * irb[0])
    vb[0, pl.ds(0, BLOCK), :] = high
    vb[0, pl.ds(BLOCK, BLOCK), :] = low
    moments = mm_t(jnp.concatenate([q0, u0], axis=0), u0)
    sum_start(1, jnp.concatenate([pack(moments[:BLOCK, :]), pack(moments[BLOCK:, :])], axis=0))
    to_partners(vb, v_sem.at[0], v_sem.at[1])
    sum_plane(1, 16)
    sum_line(1, 16)
    arrived(vb.at[others], v_sem.at[1])
    v2 = apply(vb)

    def eye():
        shape = (BLOCK, BLOCK)
        same = lax.broadcasted_iota(jnp.int32, shape, 0) == lax.broadcasted_iota(jnp.int32, shape, 1)
        return jnp.where(same, 1.0, 0.0).astype(F32)

    summed = sum_end(1, 16)
    e0 = unpack(summed[:8, :])
    e0_t = e0.T
    coef_ref[0] = e0 + eye()
    b0, inverse = factorise(unpack(summed[8:, :]) - mm(e0_t, e0))
    coef_ref[1] = b0
    pair = jnp.concatenate([u0, v2], axis=1) - mm(e0_t, jnp.concatenate([q0, w0], axis=1))
    pair = mm(inverse, pair)
    q1 = pair[:, :ROWS]
    out_ref[pl.ds(BLOCK, BLOCK), :] = q1
    u1 = pair[:, ROWS:] - mm(b0, q0) - q1
    moments = mm_t(jnp.concatenate([q1, u1], axis=0), u1)
    sum_start(2, jnp.concatenate([pack(moments[:BLOCK, :]), pack(moments[BLOCK:, :])], axis=0))
    sum_plane(2, 16)
    sum_line(2, 16)

    arrived(xb.at[pl.ds(0, PARTNERS - 1)], x_send)
    arrived(irb.at[others], ir_sem.at[0])
    arrived(vb.at[others], v_sem.at[0])
    sum_drain(0, 8)
    sum_drain(1, 16)

    summed = sum_end(2, 16)
    e1 = unpack(summed[:8, :])
    e1_t = e1.T
    coef_ref[2] = e1 + eye()
    b1, inverse = factorise(unpack(summed[8:, :]) - mm(e1_t, e1))
    coef_ref[3] = b1
    out_ref[pl.ds(2 * BLOCK, BLOCK), :] = mm(inverse, u1 - mm(e1_t, q1))
    sum_drain(2, 16)


def local(snapshots, bins, pairs, start_weights):
    rows, features = snapshots.shape
    vmem = pl.BlockSpec(memory_space=pltpu.VMEM)
    basis, coefficients = pl.pallas_call(
        kernel,
        out_shape=(
            jax.ShapeDtypeStruct((3 * BLOCK, rows), F32),
            jax.ShapeDtypeStruct((4, BLOCK, BLOCK), F32),
        ),
        in_specs=[pl.BlockSpec(memory_space=pl.ANY)] * 4,
        out_specs=(vmem, vmem),
        scratch_shapes=[
            pltpu.VMEM((bins.shape[0] // 128, 128), jnp.int32),
            pltpu.VMEM((2, pairs.shape[0]), jnp.int32),
            pltpu.VMEM(start_weights.shape[::-1], BF16),
            pltpu.VMEM((PARTNERS, rows, features), BF16),
            pltpu.VMEM((PARTNERS, rows, rows), BF16),
            pltpu.VMEM((PARTNERS, rows, rows), BF16),
            pltpu.VMEM((PARTNERS, rows, WINDOW), BF16),
            pltpu.VMEM((WINDOW, rows), BF16),
            pltpu.VMEM((BLOCK, PARTNERS * rows), F32),
            pltpu.VMEM((8, rows), F32),
            pltpu.VMEM((8, rows), F32),
            pltpu.VMEM((PARTNERS, 1, rows), F32),
            pltpu.VMEM((PARTNERS, 2 * BLOCK, rows), BF16),
            pltpu.VMEM((PARTNERS, 2 * BLOCK, rows), BF16),
            pltpu.VMEM((3, 2, 16, 128), F32),
            pltpu.VMEM((3, NX * NY, 16, 128), F32),
            pltpu.VMEM((3, NZ, 16, 128), F32),
            pltpu.SemaphoreType.DMA,
            pltpu.SemaphoreType.DMA((5, CHUNKS)),
            pltpu.SemaphoreType.DMA((5, 2)),
            pltpu.SemaphoreType.DMA((1, 1)),
            pltpu.SemaphoreType.DMA((2,)),
            pltpu.SemaphoreType.DMA((2,)),
            pltpu.SemaphoreType.DMA((3, 6)),
            pltpu.SemaphoreType.DMA((4,)),
        ],
        compiler_params=pltpu.CompilerParams(
            collective_id=0, has_side_effects=True, vmem_limit_bytes=62 << 20
        ),
    )(snapshots, bins.reshape(-1, 128), pairs.T, start_weights.T)
    return basis.T, coefficients


def solution(mesh):
    in_specs = (P(("loop", "inner"), None), P(), P(), P())
    out_specs = (P(("loop", "inner"), None), P())
    return jax.shard_map(local, mesh=mesh, in_specs=in_specs, out_specs=out_specs, check_vma=False)
```

```python
import functools

import jax
import jax.numpy as jnp
from jax import lax
from jax.experimental import pallas as pl
from jax.experimental.pallas import tpu as pltpu
from jax.sharding import PartitionSpec as P

MESH = pl.DeviceIdType.MESH
HIGHEST = lax.Precision.HIGHEST
F32 = jnp.float32
BF16 = jnp.bfloat16

NX, NY, NZ = 4, 4, 8
BINS_COL = 8
WINDOW = 32
ROWS = 256
BLOCK = 32
PARTNERS = 12
CHUNKS = 8
CHUNK = ROWS // CHUNKS
DIRECT = 3
HALF = ROWS // 2


def mm(a, b):
    return lax.dot_general(a, b, (((1,), (0,)), ((), ())), precision=HIGHEST, preferred_element_type=F32)


def mm_t(a, b):
    return lax.dot_general(a, b, (((1,), (1,)), ((), ())), precision=HIGHEST, preferred_element_type=F32)


def t_mm(a, b):
    return mm(a.T, b)


def split(v):
    high = v.astype(BF16)
    return high, (v - high.astype(F32)).astype(BF16)


def pack(m):
    return jnp.concatenate([m[8 * g : 8 * g + 8, :] for g in range(4)], axis=1)


def unpack(p):
    return jnp.concatenate([p[:, 32 * g : 32 * g + 32] for g in range(4)], axis=0)


def factorise(gram):
    sub = lax.broadcasted_iota(jnp.int32, (BLOCK, BLOCK), 0)
    lane = lax.broadcasted_iota(jnp.int32, (BLOCK, BLOCK), 1)
    eye = (sub == lane).astype(F32)
    work = jnp.concatenate([gram, eye], axis=1)
    below = lax.broadcasted_iota(jnp.int32, (BLOCK, 2 * BLOCK), 0)
    scale = jnp.zeros((BLOCK, 2 * BLOCK), F32)
    for k in range(0, BLOCK, 2):
        first = jnp.broadcast_to(work[:, k : k + 1], (BLOCK, 2 * BLOCK))
        second = jnp.broadcast_to(work[:, k + 1 : k + 2], (BLOCK, 2 * BLOCK))
        row, next_row = work[k : k + 1, :], work[k + 1 : k + 2, :]
        pivot, cross = first[k : k + 1, :], second[k : k + 1, :]
        inverse = 1.0 / pivot
        ratio = first[k + 1 : k + 2, :] * inverse
        next_row = next_row - ratio * row
        next_pivot = second[k + 1 : k + 2, :] - ratio * cross
        second = second - first * (cross * inverse)
        change = first * (row * inverse) + second * (next_row * (1.0 / next_pivot))
        scale = jnp.where(below == k, pivot, jnp.where(below == k + 1, next_pivot, scale))
        work = jnp.where(below == k + 1, next_row, work) - jnp.where(below > k + 1, change, 0.0)
    work = work * lax.rsqrt(scale)
    upper = jnp.where(lane >= sub, work[:, :BLOCK], 0.0)
    return upper, work[:, BLOCK:]


def kernel(
    x_hbm, bins_hbm, pairs_hbm, wt_hbm, out_ref, coef_ref,
    bins_ref, pairs_ref, wt_ref, xb, kh, kl, hot, links, st, sq_row, deg, irb, zb, vb, core_buf, plane_buf, line_buf,
    x_send, x_first, x_fwd, x_core, ir_sem, v_sem, ar_sem, in_sem, root_sem,
):
    x_ref = xb.at[0]
    arrivals = [
        pltpu.make_async_copy(src, dst, in_sem.at[n])
        for n, (src, dst) in enumerate(
            ((x_hbm, x_ref), (wt_hbm, wt_ref), (pairs_hbm, pairs_ref), (bins_hbm, bins_ref))
        )
    ]
    for copy in arrivals:
        copy.start()
    features = xb.shape[2]
    group = lax.axis_index("loop")
    inner = lax.axis_index("inner")
    core = group % 2
    odd = inner % 2
    y = (group // 2) * 2 + odd
    x = (inner // 2) % NX
    z = inner // (2 * NX)

    def device(c, xx, yy, zz):
        yy = yy % NY
        return ((yy // 2) * 2 + c, (zz % NZ) * (2 * NX) + (xx % NX) * 2 + yy % 2)

    def near(dc, dy, di):
        yy = (y + dy) % NY
        return ((yy // 2) * 2 + (core + dc) % 2, ((inner // 2 + di) % (NX * NZ)) * 2 + yy % 2)

    step = 1 - 2 * odd
    other = near(1, 0, 0)

    barrier = pltpu.get_barrier_semaphore()
    greeted = [other]
    greeted += [device(core, x + a, y + b, z) for a in range(NX) for b in range(NY) if a or b]
    greeted += [device(core, x, y, z + a) for a in range(1, NZ)]
    greeted += [near(1, dy, 0) for dy in (1, 2, 3)]
    greeted += [near(dc, dy, -step) for dc in (0, 1) for dy in (1, 3)]
    greeted += [near(0, 0, 1), near(0, 0, -1)]
    for d in greeted:
        pl.semaphore_signal(barrier, inc=1, device_id=d, device_id_type=MESH)
    pl.semaphore_wait(barrier, len(greeted))
    arrivals[0].wait()

    def remote(src, dst, send, recv, target):
        return pltpu.make_async_remote_copy(
            src_ref=src, dst_ref=dst, send_sem=send, recv_sem=recv, device_id=target, device_id_type=MESH
        )

    def rows_of(chunk):
        return pl.ds(chunk * CHUNK, CHUNK)

    def push(src, slot, chunk, recv, target):
        source = x_ref.at[rows_of(chunk)] if src is None else xb.at[src, rows_of(chunk)]
        remote(source, xb.at[slot, rows_of(chunk)], x_send, recv, target).start()

    def arrived(ref, sem):
        pltpu.make_async_copy(ref, ref, sem).wait()

    up = list(range(CHUNKS))
    down = up[CHUNKS // 2 :] + up[: CHUNKS // 2]
    far_up, far_down = up[CHUNKS - DIRECT :], down[CHUNKS - DIRECT :]
    for k in range(CHUNKS):
        push(None, 3, up[k], x_first.at[1, up[k]], near(0, 1, 0))
        push(None, 2, down[k], x_first.at[0, down[k]], near(0, -1, 0))
        if k < DIRECT:
            push(None, 6, far_up[k], x_first.at[4, far_up[k]], near(0, 1, -step))
            push(None, 5, far_down[k], x_first.at[3, far_down[k]], near(0, -1, -step))
    remote(x_ref, xb.at[1], x_send, x_core.at[0, 0], other).start()

    def sum_start(n, packed):
        rows = packed.shape[0]
        core_buf[n, 0, pl.ds(0, rows)] = packed
        remote(
            core_buf.at[n, 0, pl.ds(0, rows)], core_buf.at[n, 1, pl.ds(0, rows)],
            ar_sem.at[n, 0], ar_sem.at[n, 1], other,
        ).start()

    def sum_plane(n, rows):
        arrived(core_buf.at[n, 1, pl.ds(0, rows)], ar_sem.at[n, 1])
        both = core_buf[n, 0, pl.ds(0, rows)] + core_buf[n, 1, pl.ds(0, rows)]
        mine = x * NY + y
        plane_buf[n, mine, pl.ds(0, rows)] = both
        place = plane_buf.at[n, mine, pl.ds(0, rows)]

        def send(k, carry):
            remote(
                place, place, ar_sem.at[n, 2], ar_sem.at[n, 3], device(core, x + k // NY, y + k % NY, z)
            ).start()
            return carry

        lax.fori_loop(1, NX * NY, send, 0)

    def sum_line(n, rows):
        span = plane_buf.at[n, pl.ds(0, NX * NY - 1), pl.ds(0, rows)]
        arrived(span, ar_sem.at[n, 3])
        total = jnp.sum(plane_buf[n, :, pl.ds(0, rows)], axis=0)
        line_buf[n, z, pl.ds(0, rows)] = total
        place = line_buf.at[n, z, pl.ds(0, rows)]

        def send(k, carry):
            remote(place, place, ar_sem.at[n, 4], ar_sem.at[n, 5], device(core, x, y, z + k)).start()
            return carry

        lax.fori_loop(1, NZ, send, 0)

    def sum_end(n, rows):
        arrived(line_buf.at[n, pl.ds(0, NZ - 1), pl.ds(0, rows)], ar_sem.at[n, 5])
        return jnp.sum(line_buf[n, :, pl.ds(0, rows)], axis=0)

    def sum_drain(n, rows):
        arrived(core_buf.at[n, 0, pl.ds(0, rows)], ar_sem.at[n, 0])
        arrived(plane_buf.at[n, pl.ds(0, NX * NY - 1), pl.ds(0, rows)], ar_sem.at[n, 2])
        arrived(line_buf.at[n, pl.ds(0, NZ - 1), pl.ds(0, rows)], ar_sem.at[n, 4])

    for copy in arrivals[1:]:
        copy.wait()

    own = x_ref[...]
    wt = wt_ref[...]
    start = lax.dot_general(wt, own, (((1,), (1,)), ((), ())), preferred_element_type=F32)
    sum_start(0, pack(mm_t(start, start)))

    pairs = pairs_ref[...]
    left, right = pairs[0:1, :], pairs[1:2, :]
    count = pairs.shape[1]
    my_base = inner * BINS_COL
    window_base = my_base - BINS_COL

    def one_hot(values, base, width):
        ids = lax.broadcasted_iota(jnp.int32, (width, values.shape[1]), 0)
        return jnp.where(values - base == ids, 1.0, 0.0).astype(F32)

    def count_pairs(mine, theirs):
        return lax.dot_general(
            one_hot(mine, my_base, BINS_COL).astype(BF16), one_hot(theirs, window_base, WINDOW).astype(BF16),
            (((1,), (1,)), ((), ())), preferred_element_type=F32,
        )

    linked = jnp.where(count_pairs(left, right) + count_pairs(right, left) > 0.5, 1.0, 0.0)

    def bins_of(block):
        eight = bins_ref[pl.ds(pl.multiple_of((block // 4) * 8, 8), 8), :]
        which = lax.broadcasted_iota(jnp.int32, eight.shape, 0) - 2 * (block % 4)
        first = jnp.sum(jnp.where(which == 0, eight, 0), axis=0, keepdims=True)
        second = jnp.sum(jnp.where(which == 1, eight, 0), axis=0, keepdims=True)
        return jnp.concatenate([first, second], axis=1)

    n_inner = NX * NZ * 2
    my_bins = bins_of(group * n_inner + inner)
    links[...] = mm(linked.T, one_hot(my_bins, my_base, BINS_COL)).astype(BF16)

    def set_hot(slot, where, valid):
        hits = one_hot(bins_of(where[0] * n_inner + where[1]), window_base, WINDOW)
        if valid is not None:
            hits = hits * valid
        hot[slot] = hits.T.astype(BF16)

    across = jnp.where((inner == 0) | (inner == n_inner - 1), 0.0, 1.0).astype(F32)
    set_hot(0, (group, inner), None)
    set_hot(1, other, None)
    for dc in (0, 1):
        for slot, dy in ((2, 1), (3, -1), (4, 2)):
            set_hot(slot + 5 * dc, near(dc, dy, 0), None)
        for slot, dy in ((5, 1), (6, -1)):
            set_hot(slot + 5 * dc, near(dc, dy, -step), across)

    wide = own.astype(F32)
    sq_high, sq_low = split(wide * wide)
    ones = jnp.ones((16, features), BF16)
    norms = lax.dot_general(ones, sq_high, (((1,), (1,)), ((), ())), preferred_element_type=F32)
    norms = norms + lax.dot_general(ones, sq_low, (((1,), (1,)), ((), ())), preferred_element_type=F32)
    sq_row[...] = norms[0:8, :]
    deg[...] = jnp.zeros_like(deg)

    def tile(slot, half):
        span = pl.ds(pl.multiple_of(half * HALF, HALF), HALF)
        theirs = xb[slot, span, :]
        theirs_wide = theirs.astype(F32)
        their_norm = jnp.sum(theirs_wide * theirs_wide, axis=1, keepdims=True)
        products = lax.dot_general(theirs, x_ref[...], (((1,), (1,)), ((), ())), preferred_element_type=F32)
        distance = their_norm + sq_row[0:1, :] - 2.0 * products
        mask = jnp.dot(hot[slot, span, :], links[...], preferred_element_type=F32)
        value = mask * jnp.exp(distance * (-3.0 / features))
        deg[...] += jnp.sum(value.reshape(HALF // 8, 8, ROWS), axis=0)
        high, low = split(value)
        kh[slot, span, :] = high
        kl[slot, span, :] = low
        st[:, pl.ds(slot * ROWS + half * HALF, HALF)] = lax.dot_general(
            wt_ref[...], theirs, (((1,), (1,)), ((), ())), preferred_element_type=F32
        )

    def whole(slot):
        tile(slot, 0)
        tile(slot, 1)

    def forward(slot, chunk, target_slot, recv, target):
        push(slot, target_slot, chunk, recv, target)

    def got(slot, chunk):
        arrived(xb.at[slot, rows_of(chunk)], x_first.at[slot - 2, chunk])

    def to_core(slot, half):
        span = pl.ds(half * HALF, HALF)
        remote(xb.at[slot, span], xb.at[slot + 5, span], x_send, x_fwd.at[slot - 2, half], other).start()

    def got_core(slot, half):
        arrived(xb.at[slot, pl.ds(half * HALF, HALF)], x_fwd.at[slot - 7, half])

    sum_plane(0, 8)
    whole(0)
    arrived(xb.at[1], x_core.at[0, 0])
    whole(1)

    per = CHUNKS // 2
    for k in range(CHUNKS):
        a, b = down[k], up[k]
        got(2, a)
        if k < CHUNKS - DIRECT:
            push(2, 5, a, x_first.at[3, a], near(0, 0, step))
        if k < per:
            push(2, 4, a, x_first.at[2, a], near(0, -1, 0))
        got(3, b)
        if k < CHUNKS - DIRECT:
            push(3, 6, b, x_first.at[4, b], near(0, 0, step))
        if k < per:
            push(3, 4, b, x_first.at[2, b], near(0, 1, 0))
        if k % per == per - 1:
            to_core(2, a // per)
            to_core(3, b // per)
            tile(2, a // per)
            tile(3, b // per)
    sum_line(0, 8)
    for h in (0, 1):
        for s, halves in ((7, (1, 0)), (8, (0, 1))):
            got_core(s, halves[h])
            tile(s, halves[h])
    for h in (0, 1):
        for chunk in range(per * h, per * h + per):
            got(4, chunk)
        to_core(4, h)
        tile(4, h)
    for h in (0, 1):
        for s, halves in ((5, (1, 0)), (6, (0, 1))):
            for chunk in range(per * halves[h], per * halves[h] + per):
                got(s, chunk)
            to_core(s, halves[h])
            tile(s, halves[h])
        got_core(9, h)
        tile(9, h)
    for h in (0, 1):
        for s, halves in ((10, (1, 0)), (11, (0, 1))):
            got_core(s, halves[h])
            tile(s, halves[h])

    degree = jnp.sum(deg[...], axis=0, keepdims=True)
    root = lax.rsqrt(degree)
    irb[0] = root

    def to_partners(buf, send, recv):
        place = buf.at[0]

        def to(slot, target):
            remote(place, buf.at[slot], send, recv(slot), target).start()

        for dc in (1, 0):
            for slot, dy in ((6, 1), (5, -1)):
                to(slot + 5 * dc, near(dc, dy, -step))
        for dc in (1, 0):
            for slot, dy in ((4, 2), (3, 1), (2, -1)):
                to(slot + 5 * dc, near(dc, dy, 0))
        to(1, other)

    others = pl.ds(1, PARTNERS - 1)
    to_partners(irb, ir_sem.at[0], lambda slot: root_sem.at[slot])

    unused, inverse = factorise(unpack(sum_end(0, 8)))
    st[...] = mm(inverse, st[...])
    q0 = st[:, pl.ds(0, ROWS)]
    out_ref[pl.ds(0, BLOCK), :] = q0


    def apply(buf, arrive):
        total = jnp.zeros((2 * BLOCK, ROWS), F32)
        rest = jnp.zeros((BLOCK, ROWS), F32)
        for slot in (0, 1, 2, 3, 7, 8, 4, 9, 5, 6, 10, 11):
            arrive(slot)
            vectors = buf[slot]
            total = total + jnp.dot(vectors, kh[slot], preferred_element_type=F32)
            rest = rest + jnp.dot(vectors[:BLOCK, :], kl[slot], preferred_element_type=F32)
        return (total[:BLOCK, :] + (total[BLOCK:, :] + rest)) * irb[0]

    def scale_start(slot):
        if slot > 0:
            arrived(irb.at[slot], root_sem.at[slot])
        high, low = split(st[:, pl.ds(slot * ROWS, ROWS)] * irb[slot])
        zb[slot, pl.ds(0, BLOCK), :] = high
        zb[slot, pl.ds(BLOCK, BLOCK), :] = low

    w0 = apply(zb, scale_start)
    u0 = w0 - q0
    high, low = split(u0 * irb[0])
    vb[0, pl.ds(0, BLOCK), :] = high
    vb[0, pl.ds(BLOCK, BLOCK), :] = low
    moments = mm_t(jnp.concatenate([q0, u0], axis=0), u0)
    sum_start(1, jnp.concatenate([pack(moments[:BLOCK, :]), pack(moments[BLOCK:, :])], axis=0))
    to_partners(vb, v_sem.at[0], lambda slot: v_sem.at[1])
    sum_plane(1, 16)
    sum_line(1, 16)
    arrived(vb.at[others], v_sem.at[1])
    v2 = apply(vb, lambda slot: None)

    def eye():
        shape = (BLOCK, BLOCK)
        same = lax.broadcasted_iota(jnp.int32, shape, 0) == lax.broadcasted_iota(jnp.int32, shape, 1)
        return jnp.where(same, 1.0, 0.0).astype(F32)

    summed = sum_end(1, 16)
    e0 = unpack(summed[:8, :])
    e0_t = e0.T
    coef_ref[0] = e0 + eye()
    b0, inverse = factorise(unpack(summed[8:, :]) - mm(e0_t, e0))
    coef_ref[1] = b0
    pair = jnp.concatenate([u0, v2], axis=1) - mm(e0_t, jnp.concatenate([q0, w0], axis=1))
    pair = mm(inverse, pair)
    q1 = pair[:, :ROWS]
    out_ref[pl.ds(BLOCK, BLOCK), :] = q1
    u1 = pair[:, ROWS:] - mm(b0, q0) - q1
    moments = mm_t(jnp.concatenate([q1, u1], axis=0), u1)
    sum_start(2, jnp.concatenate([pack(moments[:BLOCK, :]), pack(moments[BLOCK:, :])], axis=0))
    sum_plane(2, 16)
    sum_line(2, 16)

    arrived(xb.at[pl.ds(0, PARTNERS - 1)], x_send)
    arrived(irb.at[others], ir_sem.at[0])
    arrived(vb.at[others], v_sem.at[0])
    sum_drain(0, 8)
    sum_drain(1, 16)

    summed = sum_end(2, 16)
    e1 = unpack(summed[:8, :])
    e1_t = e1.T
    coef_ref[2] = e1 + eye()
    b1, inverse = factorise(unpack(summed[8:, :]) - mm(e1_t, e1))
    coef_ref[3] = b1
    out_ref[pl.ds(2 * BLOCK, BLOCK), :] = mm(inverse, u1 - mm(e1_t, q1))
    sum_drain(2, 16)


def local(snapshots, bins, pairs, start_weights):
    rows, features = snapshots.shape
    vmem = pl.BlockSpec(memory_space=pltpu.VMEM)
    basis, coefficients = pl.pallas_call(
        kernel,
        out_shape=(
            jax.ShapeDtypeStruct((3 * BLOCK, rows), F32),
            jax.ShapeDtypeStruct((4, BLOCK, BLOCK), F32),
        ),
        in_specs=[pl.BlockSpec(memory_space=pl.ANY)] * 4,
        out_specs=(vmem, vmem),
        scratch_shapes=[
            pltpu.VMEM((bins.shape[0] // 128, 128), jnp.int32),
            pltpu.VMEM((2, pairs.shape[0]), jnp.int32),
            pltpu.VMEM(start_weights.shape[::-1], BF16),
            pltpu.VMEM((PARTNERS, rows, features), BF16),
            pltpu.VMEM((PARTNERS, rows, rows), BF16),
            pltpu.VMEM((PARTNERS, rows, rows), BF16),
            pltpu.VMEM((PARTNERS, rows, WINDOW), BF16),
            pltpu.VMEM((WINDOW, rows), BF16),
            pltpu.VMEM((BLOCK, PARTNERS * rows), F32),
            pltpu.VMEM((8, rows), F32),
            pltpu.VMEM((8, rows), F32),
            pltpu.VMEM((PARTNERS, 1, rows), F32),
            pltpu.VMEM((PARTNERS, 2 * BLOCK, rows), BF16),
            pltpu.VMEM((PARTNERS, 2 * BLOCK, rows), BF16),
            pltpu.VMEM((3, 2, 16, 128), F32),
            pltpu.VMEM((3, NX * NY, 16, 128), F32),
            pltpu.VMEM((3, NZ, 16, 128), F32),
            pltpu.SemaphoreType.DMA,
            pltpu.SemaphoreType.DMA((5, CHUNKS)),
            pltpu.SemaphoreType.DMA((5, 2)),
            pltpu.SemaphoreType.DMA((1, 1)),
            pltpu.SemaphoreType.DMA((2,)),
            pltpu.SemaphoreType.DMA((2,)),
            pltpu.SemaphoreType.DMA((3, 6)),
            pltpu.SemaphoreType.DMA((4,)),
            pltpu.SemaphoreType.DMA((PARTNERS,)),
        ],
        compiler_params=pltpu.CompilerParams(
            collective_id=0, has_side_effects=True, vmem_limit_bytes=62 << 20
        ),
    )(snapshots, bins.reshape(-1, 128), pairs.T, start_weights.T)
    return basis.T, coefficients


def solution(mesh):
    in_specs = (P(("loop", "inner"), None), P(), P(), P())
    out_specs = (P(("loop", "inner"), None), P())
    return jax.shard_map(local, mesh=mesh, in_specs=in_specs, out_specs=out_specs, check_vma=False)
```
